512 devices in a mesh: chan: 128 (over x, z, core), tm: 4 (over y).
Axes of the slice: x: 4, y: 4, z: 16, core: 2. Of those that a mesh axis runs over, the one named last changes fastest.
Arguments:
- voltages: bfloat16 [2, 1024, 262144], P(None, 'chan', 'tm'), may hold values from -6 to 6
- flags: int32 [512, 64], P('chan', 'tm'), may hold values 0 or 1
- pairs: int32 [2, 2], replicated, may hold values from 0 to 15
Outputs:
- visibilities: float32 [4096, 2, 64, 128], P(('chan', 'tm'))
The draws below stay inside these ranges and needn't reach their ends.
All inputs are finite; a program needn't handle non-finite values. No bound on the sum of `flags` on one device may be relied on, other than what follows from the above.
Results may differ from the reference program's by a relative error of at most 0.0082.
Values may be sent and summed in bfloat16 or wider, within the bound.
A program may use at most 128 MiB of HBM per device.

```python
import math
import jax
import jax.numpy as jnp
from jax import lax

INPUTS = 1024
STATIONS = 512
CHANNELS = 4096
TAPS = 16
BLOCK = 64
BLOCKS = 16
FRAMES = 64
SAMPLES = 262144
LISTED = 2


def touch_ends(array, stream_key, smallest, largest):
    index_at = [jax.random.randint(jax.random.fold_in(stream_key, axis), (), 0, length) for axis, length in enumerate(array.shape)]
    longest = array.shape.index(max(array.shape))
    next_to = index_at[:longest] + [(index_at[longest] + 1) % array.shape[longest]] + index_at[longest + 1:]
    return array.at[tuple(index_at)].set(smallest).at[tuple(next_to)].set(largest)


def block_scale(key, dims, cuts, least, top_value):
    level = 1.0
    for dim, shards_of in cuts:
        steps = jax.random.uniform(jax.random.fold_in(jax.random.fold_in(key, 6), dim), (shards_of,), jnp.float32, least / len(cuts), top_value / len(cuts))
        level = level * jnp.repeat(jnp.exp(steps), dims[dim] // shards_of).reshape((-1,) + (1,) * (len(dims) - 1 - dim))
    return level


def bell_draw(stream_key, shape, spread, most, cuts=(), held_as=jnp.bfloat16):
    entries = spread * jax.random.normal(stream_key, shape, jnp.float32)
    if cuts:
        entries = entries * block_scale(stream_key, shape, cuts, -0.22, 0.18)
    return jnp.clip(entries, -most, most).astype(held_as)


def setup_inputs(seed: int = 0) -> dict:
    key_list = jax.random.split(jax.random.key(seed), 4)
    return {
        "voltages": bell_draw(key_list[0], (2, INPUTS, SAMPLES), 1.0, 6.0, ((1, 128), (2, 4))),
        "flags": touch_ends((jax.random.randint(key_list[1], (STATIONS, FRAMES), 0, 4) < 3).astype(jnp.int32), jax.random.fold_in(key_list[1], 1), 0, 1),
        "pairs": touch_ends(jax.random.randint(key_list[2], (LISTED, 2), 0, BLOCKS), jax.random.fold_in(key_list[2], 1), 0, BLOCKS - 1).astype(jnp.int32),
    }


def window_table():
    length = TAPS * CHANNELS
    index = jnp.arange(length).astype(jnp.float32)
    offset = (index - length / 2 + 0.5) / CHANNELS
    taper = 0.5 - 0.5 * jnp.cos(2.0 * math.pi * (index + 0.5) / length)
    return (jnp.sinc(offset) * taper).reshape(TAPS, CHANNELS)

def dft_table(order, factor):
    counts = jnp.arange(order)
    angle = (counts[:, None] * counts[None, :] % order).astype(jnp.float32) * (2.0 * math.pi / order)
    cosine = jnp.cos(angle) * factor
    sine = jnp.sin(angle) * factor
    upper = jnp.stack([cosine, -sine], axis=1)
    lower = jnp.stack([sine, cosine], axis=1)
    return jnp.stack([upper, lower], axis=0)

def analyse(extended, live_mask):
    frames = extended.shape[2] - (TAPS - 1)
    inner = CHANNELS // 16
    window = window_table()
    total = jnp.zeros((2, extended.shape[1], frames, CHANNELS), jnp.float32)
    for step in range(TAPS):
        total = total + window[step] * extended[:, :, step:step + frames, :].astype(jnp.float32)
    filtered = total.astype(jnp.bfloat16)
    pieces = filtered.reshape(2, extended.shape[1], frames, 16, inner)
    first = dft_table(16, 0.25).astype(jnp.bfloat16)
    partial_value = jnp.einsum('rgfnq,rnsk->gfksq', pieces.astype(jnp.float32), first.astype(jnp.float32))
    coarse = jnp.arange(16)
    fine_idx = jnp.arange(inner)
    angle = (coarse[:, None] * fine_idx[None, :]).astype(jnp.float32) * (2.0 * math.pi / CHANNELS)
    cosine = jnp.cos(angle)
    sine = jnp.sin(angle)
    real_part = partial_value[:, :, :, 0, :]
    imag_part = partial_value[:, :, :, 1, :]
    rot_real = real_part * cosine + imag_part * sine
    rot_imag = imag_part * cosine - real_part * sine
    rotated = jnp.stack([rot_real, rot_imag], axis=3).astype(jnp.bfloat16)
    rotated = rotated.reshape(extended.shape[1], frames, 16, 2 * inner)
    second = dft_table(inner, 1.0 / math.sqrt(inner)).astype(jnp.bfloat16).reshape(2 * inner, 2, inner)
    spectrum = jnp.einsum('gfkn,nrq->qkrfg', rotated.astype(jnp.float32), second.astype(jnp.float32))
    spectrum = spectrum * jnp.transpose(live_mask)
    return spectrum.astype(jnp.bfloat16).reshape(CHANNELS, 2, frames, extended.shape[1])

def correlate(left_block, right_block, norm_scale):
    count = left_block.shape[0]
    rows_all = 2 * left_block.shape[2]
    a_side = left_block.reshape(count, rows_all, BLOCK).astype(jnp.float32)
    b_real = right_block.reshape(count, rows_all, BLOCK)
    b_imag = jnp.concatenate([-right_block[:, 1], right_block[:, 0]], axis=1)
    b_side = jnp.concatenate([b_real, b_imag], axis=2).astype(jnp.float32)
    return jnp.einsum('cxi,cxj->cij', a_side, b_side) * norm_scale

def reference(voltages, flags, pairs):
    frames_all = voltages.shape[2] // CHANNELS
    live_all = jnp.repeat(flags, 2, axis=0).astype(jnp.float32)

    def one_block(block_index):
        start = (block_index * BLOCK).astype(jnp.int32)
        piece = lax.dynamic_slice_in_dim(voltages, start, BLOCK, 1)
        piece = piece.reshape(2, BLOCK, frames_all, CHANNELS)
        piece = jnp.pad(piece, ((0, 0), (0, 0), (TAPS - 1, 0), (0, 0)))
        live_mask = lax.dynamic_slice_in_dim(live_all, start, BLOCK, 0)
        return analyse(piece, live_mask)
    spectra = lax.map(one_block, jnp.arange(BLOCKS).astype(jnp.int32))

    def one_pair(block_pair):
        left_block = lax.dynamic_index_in_dim(spectra, block_pair[0].astype(jnp.int32), 0, keepdims=False)
        right_block = lax.dynamic_index_in_dim(spectra, block_pair[1].astype(jnp.int32), 0, keepdims=False)
        return correlate(left_block, right_block, 1.0 / frames_all)
    result = lax.map(one_pair, pairs)
    return jnp.transpose(result, (1, 0, 2, 3))
```

```python
import functools
import math

import jax
import jax.numpy as jnp
import ml_dtypes
import numpy as np
from jax import lax
from jax.experimental import pallas as pl
from jax.experimental.pallas import tpu as pltpu
from jax.sharding import PartitionSpec as P

CHANNELS = 4096
TAPS = 16
BLOCK = 64
NX, NZ, NC, NY = 4, 16, 2, 4
LOCAL = 16
FRAMES = 64
INNER = 256
MESH = pl.DeviceIdType.MESH


def window_table():
    length = TAPS * CHANNELS
    index = np.arange(length, dtype=np.float64)
    offset = (index - length / 2 + 0.5) / CHANNELS
    taper = 0.5 - 0.5 * np.cos(2.0 * math.pi * (index + 0.5) / length)
    return (np.sinc(offset) * taper).astype(np.float32).reshape(TAPS, 16, INNER)


def dft_table(order, factor):
    counts = np.arange(order)
    angle = (counts[:, None] * counts[None, :] % order).astype(np.float64) * (2.0 * math.pi / order)
    cosine = np.cos(angle) * factor
    sine = np.sin(angle) * factor
    upper = np.stack([cosine, -sine], axis=1)
    lower = np.stack([sine, cosine], axis=1)
    table = np.stack([upper, lower], axis=0)
    return table.astype(np.float32).astype(ml_dtypes.bfloat16)


def first_table():
    first = dft_table(16, 0.25).astype(np.float32)
    table = np.zeros((2, 16, 8, 8, 2, 16), np.float32)
    for f in range(8):
        table[:, :, f, f] = first.transpose(2, 3, 0, 1)
    return table.reshape(256, 256).astype(ml_dtypes.bfloat16)


def twiddle_tables():
    angle = np.arange(16)[:, None] * np.arange(INNER)[None, :] * (2.0 * math.pi / CHANNELS)
    angle = np.repeat(angle, 8, axis=0)
    return np.cos(angle).astype(np.float32), np.sin(angle).astype(np.float32)


def second_table():
    second = dft_table(INNER, 1.0 / math.sqrt(INNER))
    second = second.transpose(3, 2, 0, 1).reshape(NX, NZ, NC, 2, 2, 2 * INNER)
    return np.ascontiguousarray(second.transpose(0, 2, 3, 4, 1, 5)).reshape(2 * INNER, 2 * INNER)


def place():
    chan = lax.axis_index("chan")
    return (
        lax.div(chan, NZ * NC),
        lax.rem(lax.div(chan, NC), NZ),
        lax.rem(chan, NC),
        lax.axis_index("tm"),
    )


def device(x, z, c, y):
    return ((x * NZ + z) * NC + c, y)


def plan_kernel(pairs_ref, plan_ref):
    zero, one = jnp.int32(0), jnp.int32(1)
    block = [pairs_ref[s // 2, s % 2] for s in range(4)]
    across = [lax.div(b, 4) for b in block]
    quarter = [lax.rem(b, 4) for b in block]
    fresh, order = [], []
    for s in range(4):
        new, spot = one, zero
        for e in range(s):
            spot = spot + jnp.where(quarter[e] == quarter[s], fresh[e], zero)
        for e in range(s):
            same = block[e] == block[s]
            spot = jnp.where(same, order[e], spot)
            new = jnp.where(same, zero, new)
        fresh.append(new)
        order.append(spot)
    most = zero
    for q in range(4):
        count = zero
        for s in range(4):
            count = count + jnp.where(quarter[s] == q, fresh[s], zero)
        most = jnp.maximum(most, count)
        for m in range(4):
            pick = zero
            for s in range(4):
                hit = (quarter[s] == q) & (order[s] == m)
                pick = jnp.where(hit, across[s], pick)
            plan_ref[4 * q + m] = pick
    for s in range(4):
        plan_ref[16 + s] = quarter[s]
        plan_ref[20 + s] = order[s]
    plan_ref[24] = most - 1


def front_kernel(
    volts, flags, window, first, cosine, sine, second,
    turned,
    line, marks, filtered, spectra,
    y_send, y_recv, f_send, f_recv, x_send, x_recv, own,
):
    x, z, c, y = place()
    barrier = pltpu.get_barrier_semaphore()
    y_peers = [(d, lax.rem(y + d, NY)) for d in (1, 3, 2)]
    x_peers = [
        (2 * dx + dc, lax.rem(x + dx, NX), lax.rem(c + dc, NC))
        for dx in (2, 1, 3, 0)
        for dc in (0, 1)
        if dx + dc > 0
    ]
    for _, other in y_peers:
        pl.semaphore_signal(barrier, inc=1, device_id=device(x, z, c, other), device_id_type=MESH)
    for _, ox, oc in x_peers:
        pl.semaphore_signal(barrier, inc=1, device_id=device(ox, z, oc, y), device_id_type=MESH)
    pl.semaphore_wait(barrier, len(y_peers) + len(x_peers))

    here = pl.ds(LOCAL + LOCAL * y, LOCAL)
    incoming = [[], []]
    for d, other in y_peers:
        copy = pltpu.make_async_remote_copy(
            src_ref=flags.at[other], dst_ref=marks.at[y],
            send_sem=f_send.at[d - 1], recv_sem=f_recv.at[d - 1],
            device_id=device(x, z, c, other), device_id_type=MESH,
        )
        copy.start()
        incoming[0].append(copy)
    mine = pltpu.make_async_copy(flags.at[y], marks.at[y], own.at[4])
    mine.start()
    kept = [[mine], []]
    for j in range(2):
        for d, other in y_peers:
            copy = pltpu.make_async_remote_copy(
                src_ref=volts.at[2 * other + j], dst_ref=line.at[j, :, here],
                send_sem=y_send.at[j, d - 1], recv_sem=y_recv.at[j, d - 1],
                device_id=device(x, z, c, other), device_id_type=MESH,
            )
            copy.start()
            incoming[j].append(copy)
        mine = pltpu.make_async_copy(volts.at[2 * y + j], line.at[j, :, here], own.at[j])
        mine.start()
        kept[j].append(mine)

    line[:, :, 0:LOCAL] = jnp.zeros((2, 2, LOCAL, 16, INNER), jnp.bfloat16)

    outgoing = []
    for j in range(2):
        for copy in incoming[j]:
            copy.wait_recv()
        for copy in kept[j]:
            copy.wait()

        for half in range(2):
            lanes = slice(128 * half, 128 * half + 128)

            def sift(step, _, j=j, lanes=lanes):
                p = lax.div(step, 8)
                base = lax.rem(step, 8) * 8
                taps = [window[t, :, lanes] for t in range(TAPS)]
                total = [None] * 8
                for u in range(8 + TAPS - 1):
                    value = line[j, p, base + 1 + u, :, lanes].astype(jnp.float32)
                    for g in range(8):
                        t = u - g
                        if 0 <= t < TAPS:
                            term = taps[t] * value
                            total[g] = term if t == 0 else total[g] + term
                for g in range(8):
                    filtered[base + g, p, :, lanes] = total[g].astype(jnp.bfloat16)
                return 0

            lax.fori_loop(0, 16, sift, 0)

        def transform(part, _, j=j):
            reals, imags = [], []
            for half in range(2):
                block = filtered[pl.ds(part * LOCAL + 8 * half, 8)].reshape(256, INNER)
                value = jnp.dot(first[...], block, preferred_element_type=jnp.float32)
                real, imag = value[:128], value[128:]
                rot_real = real * cosine[...] + imag * sine[...]
                rot_imag = imag * cosine[...] - real * sine[...]
                reals.append(rot_real.reshape(16, 8, INNER))
                imags.append(rot_imag.reshape(16, 8, INNER))
            real = jnp.concatenate(reals, axis=1).reshape(256, INNER)
            imag = jnp.concatenate(imags, axis=1).reshape(256, INNER)
            rotated = jnp.concatenate([real, imag], axis=1).astype(jnp.bfloat16)
            out = lax.dot_general(
                second[...], rotated, (((1,), (1,)), ((), ())), preferred_element_type=jnp.float32
            )
            live = marks[part][0:1].astype(jnp.float32)
            out = out * jnp.concatenate([live, live], axis=1)
            out = out.astype(jnp.bfloat16).reshape(NX, NC, 2, 2, NZ, 256)
            for yy in range(NY):
                low = 128 * (yy % 2)
                spectra[j, :, :, yy, part] = out[:, :, yy // 2, :, :, low : low + 128]
            return 0

        lax.fori_loop(0, 4, transform, 0)

        for k, ox, oc in x_peers:
            copy = pltpu.make_async_remote_copy(
                src_ref=spectra.at[j, ox, oc], dst_ref=turned.at[j, x, c],
                send_sem=x_send.at[j, k - 1], recv_sem=x_recv.at[j, k - 1],
                device_id=device(ox, z, oc, y), device_id_type=MESH,
            )
            copy.start()
            outgoing.append(copy)
        mine = pltpu.make_async_copy(spectra.at[j, x, c], turned.at[j, x, c], own.at[2 + j])
        mine.start()
        kept[j] = [mine]

    for copies in incoming:
        for copy in copies:
            copy.wait_send()
    for copy in outgoing:
        copy.wait_recv()
        copy.wait_send()
    for j in range(2):
        kept[j][0].wait()


def back_kernel(count, plan, turned, result, board, ready, landed, send_sem, recv_sem):
    x, z, c, y = place()
    zh, zl = lax.div(z, 4), lax.rem(z, 4)
    barrier = pltpu.get_barrier_semaphore()
    peers = NZ * NY

    def partner(step):
        return lax.rem(z + lax.div(step, NY), NZ), lax.rem(y + lax.rem(step, NY), NY)

    def greet(step, _):
        oz, oy = partner(step)
        pl.semaphore_signal(barrier, inc=1, device_id=device(x, oz, c, oy), device_id_type=MESH)
        return 0

    lax.fori_loop(1, peers, greet, 0)

    for m in range(count):
        which = plan[zh * 4 + m]

        def regroup(step, _, m=m, which=which):
            core, yy = lax.div(step, NY), lax.rem(step, NY)
            for j in range(2):
                piece = turned[j, which, core, yy].astype(jnp.float32)
                board[pl.ds(128 * j, 128), :] = piece.reshape(128, 128)
            for oz in range(NZ):
                rows = board[pl.ds(oz, 16, stride=16), :]
                ready[oz * NY + yy, m, core] = rows.astype(jnp.bfloat16)
            return 0

        lax.fori_loop(0, NC * NY, regroup, 0)

    pl.semaphore_wait(barrier, peers - 1)

    def send(step, _):
        oz, oy = partner(step)
        pltpu.make_async_remote_copy(
            src_ref=ready.at[oz * NY + oy], dst_ref=landed.at[zh, zl, :, :, y],
            send_sem=send_sem, recv_sem=recv_sem,
            device_id=device(x, oz, c, oy), device_id_type=MESH,
        ).start()
        return 0

    lax.fori_loop(1, peers, send, 0)
    pltpu.make_async_copy(ready.at[z * NY + y], landed.at[zh, zl, :, :, y], recv_sem).start()
    pltpu.make_async_copy(landed, landed, recv_sem).wait()
    sent = ready.at[pl.ds(0, peers - 1)]
    pltpu.make_async_copy(sent, sent, send_sem).wait()

    lane = lax.broadcasted_iota(jnp.int32, (1, 128), 1)

    def side(slot):
        quarter, spot = plan[16 + slot], plan[20 + slot]
        value = landed[quarter, :, spot].astype(jnp.float32)
        board[...] = value.reshape(512, 128)
        return [[board[pl.ds(2 * g + part, 64, stride=8), :] for g in range(4)] for part in range(2)]

    for b in range(2):
        left = side(2 * b)
        lefts = []
        for channel in range(8):
            keep = (lax.div(lane, 16) == channel).astype(jnp.float32)
            lefts.append(
                jnp.concatenate([(v * keep).astype(jnp.bfloat16) for v in left[0] + left[1]], axis=1)
            )
        left = jnp.concatenate(lefts, axis=0)
        right = side(2 * b + 1)
        upper = jnp.concatenate(right[0] + right[1], axis=1)
        lower = jnp.concatenate([-v for v in right[1]] + right[0], axis=1)
        right = jnp.concatenate([upper, lower], axis=0).astype(jnp.bfloat16)
        value = lax.dot_general(
            left, right, (((1,), (1,)), ((), ())), preferred_element_type=jnp.float32
        )
        result[:, b] = (value * (1.0 / FRAMES)).reshape(8, BLOCK, 2 * BLOCK)


def vmem():
    return pl.BlockSpec(memory_space=pltpu.VMEM)


def smem():
    return pl.BlockSpec(memory_space=pltpu.SMEM)


def front(volts, flags):
    bf16 = jnp.bfloat16
    cosine, sine = twiddle_tables()
    return pl.pallas_call(
        front_kernel,
        out_shape=jax.ShapeDtypeStruct((2, NX, NC, NY, 4, 2, NZ, 128), bf16),
        in_specs=[vmem()] * 7,
        out_specs=vmem(),
        scratch_shapes=[
            pltpu.VMEM((2, 2, LOCAL + FRAMES, 16, INNER), bf16),
            pltpu.VMEM((NY, 16, 128), bf16),
            pltpu.VMEM((FRAMES, 2, 16, INNER), bf16),
            pltpu.VMEM((2, NX, NC, NY, 4, 2, NZ, 128), bf16),
            pltpu.SemaphoreType.DMA((2, 3)),
            pltpu.SemaphoreType.DMA((2, 3)),
            pltpu.SemaphoreType.DMA((3,)),
            pltpu.SemaphoreType.DMA((3,)),
            pltpu.SemaphoreType.DMA((2, 7)),
            pltpu.SemaphoreType.DMA((2, 7)),
            pltpu.SemaphoreType.DMA((5,)),
        ],
        compiler_params=pltpu.CompilerParams(
            collective_id=0, has_side_effects=True, vmem_limit_bytes=40 << 20
        ),
        name="front",
    )(
        volts, flags, jnp.asarray(window_table()), jnp.asarray(first_table()),
        jnp.asarray(cosine), jnp.asarray(sine), jnp.asarray(second_table()),
    )


def back(count, plan, turned):
    bf16 = jnp.bfloat16
    return pl.pallas_call(
        functools.partial(back_kernel, count),
        out_shape=jax.ShapeDtypeStruct((8, 2, BLOCK, 2 * BLOCK), jnp.float32),
        in_specs=[smem(), vmem()],
        out_specs=vmem(),
        scratch_shapes=[
            pltpu.VMEM((512, 128), jnp.float32),
            pltpu.VMEM((NZ * NY, count, NC, 16, 128), bf16),
            pltpu.VMEM((4, 4, count, NC, NY, 16, 128), bf16),
            pltpu.SemaphoreType.DMA,
            pltpu.SemaphoreType.DMA,
        ],
        compiler_params=pltpu.CompilerParams(
            collective_id=count, has_side_effects=True, vmem_limit_bytes=40 << 20
        ),
        name="back",
    )(plan, turned)


def local(voltages, flags, pairs):
    plan = pl.pallas_call(
        plan_kernel,
        out_shape=jax.ShapeDtypeStruct((32,), jnp.int32),
        in_specs=[smem()],
        out_specs=smem(),
        name="plan",
    )(pairs)
    volts = voltages.reshape(2, 8, LOCAL, 16, INNER).transpose(1, 0, 2, 3, 4)
    live = jnp.tile(flags.astype(jnp.bfloat16), (1, 8))
    live = jnp.broadcast_to(live[:, None, :], (NY, 16, 128))
    turned = front(volts, live)
    return lax.switch(plan[24], [functools.partial(back, m) for m in range(1, 5)], plan, turned)


def solution(mesh):
    placed = (P(None, "chan", "tm"), P("chan", "tm"), P())
    return jax.shard_map(
        local,
        mesh=mesh,
        in_specs=placed,
        out_specs=P(("chan", "tm"), None, None, None),
        check_vma=False,
    )
```

```python
import functools
import math

import jax
import jax.numpy as jnp
import ml_dtypes
import numpy as np
from jax import lax
from jax.experimental import pallas as pl
from jax.experimental.pallas import tpu as pltpu
from jax.sharding import PartitionSpec as P

CHANNELS = 4096
TAPS = 16
BLOCK = 64
NX, NZ, NC, NY = 4, 16, 2, 4
LOCAL = 16
FRAMES = 64
INNER = 256
MESH = pl.DeviceIdType.MESH


def window_table():
    length = TAPS * CHANNELS
    index = np.arange(length, dtype=np.float64)
    offset = (index - length / 2 + 0.5) / CHANNELS
    taper = 0.5 - 0.5 * np.cos(2.0 * math.pi * (index + 0.5) / length)
    return (np.sinc(offset) * taper).astype(np.float32).reshape(TAPS, 16, INNER)


def dft_table(order, factor):
    counts = np.arange(order)
    angle = (counts[:, None] * counts[None, :] % order).astype(np.float64) * (2.0 * math.pi / order)
    cosine = np.cos(angle) * factor
    sine = np.sin(angle) * factor
    upper = np.stack([cosine, -sine], axis=1)
    lower = np.stack([sine, cosine], axis=1)
    table = np.stack([upper, lower], axis=0)
    return table.astype(np.float32).astype(ml_dtypes.bfloat16)


def first_table():
    first = dft_table(16, 0.25).astype(np.float32)
    table = np.zeros((2, 16, 8, 8, 2, 16), np.float32)
    for f in range(8):
        table[:, :, f, f] = first.transpose(2, 3, 0, 1)
    return table.reshape(256, 256).astype(ml_dtypes.bfloat16)


def twiddle_tables():
    angle = np.arange(16)[:, None] * np.arange(INNER)[None, :] * (2.0 * math.pi / CHANNELS)
    angle = np.repeat(angle, 8, axis=0)
    return np.cos(angle).astype(np.float32), np.sin(angle).astype(np.float32)


def second_table():
    second = dft_table(INNER, 1.0 / math.sqrt(INNER))
    second = second.transpose(3, 2, 0, 1).reshape(NX, NZ, NC, 2, 2, 2 * INNER)
    return np.ascontiguousarray(second.transpose(0, 2, 3, 4, 1, 5)).reshape(2 * INNER, 2 * INNER)


def place():
    chan = lax.axis_index("chan")
    return (
        lax.div(chan, NZ * NC),
        lax.rem(lax.div(chan, NC), NZ),
        lax.rem(chan, NC),
        lax.axis_index("tm"),
    )


def device(x, z, c, y):
    return ((x * NZ + z) * NC + c, y)


def plan_kernel(pairs_ref, plan_ref, rounds_ref):
    zero, one = jnp.int32(0), jnp.int32(1)
    block = [pairs_ref[s // 2, s % 2] for s in range(4)]
    across = [lax.div(b, 4) for b in block]
    quarter = [lax.rem(b, 4) for b in block]
    fresh, order = [], []
    for s in range(4):
        new, spot = one, zero
        for e in range(s):
            spot = spot + jnp.where(quarter[e] == quarter[s], fresh[e], zero)
        for e in range(s):
            same = block[e] == block[s]
            spot = jnp.where(same, order[e], spot)
            new = jnp.where(same, zero, new)
        fresh.append(new)
        order.append(spot)
    most = zero
    for q in range(4):
        count = zero
        for s in range(4):
            count = count + jnp.where(quarter[s] == q, fresh[s], zero)
        most = jnp.maximum(most, count)
        for m in range(4):
            pick = zero
            for s in range(4):
                hit = (quarter[s] == q) & (order[s] == m)
                pick = jnp.where(hit, across[s], pick)
            plan_ref[4 * q + m] = pick
    for s in range(4):
        plan_ref[16 + s] = quarter[s]
        plan_ref[20 + s] = order[s]
    rounds_ref[0] = most - 1


def whole_kernel(
    count, plan, volts_in, flags, window_in, first_in, cosine_in, sine_in, second_in,
    result,
    volts, window, first, cosine, sine, second,
    stage, line, live, marks, filtered, spectra,
    t0, t1, t2, t3, t4, t5, t6, t7,
    board, pairing, ready, landed_a, landed_b,
    in_sem, f_send, f_recv, y_send, y_recv, x_send, x_recv, z_send, z_recv,
):
    turned = ((t0, t1, t2, t3), (t4, t5, t6, t7))
    landed = (landed_a, landed_b)
    x, z, c, y = place()
    zh, zl = lax.div(z, 4), lax.rem(z, 4)
    peers = NZ * NY

    loads = [
        pltpu.make_async_copy(source, target, in_sem.at[i])
        for i, (source, target) in enumerate(
            [
                (volts_in, volts), (window_in, window), (first_in, first),
                (cosine_in, cosine), (sine_in, sine), (second_in, second),
            ]
        )
    ]
    for load in loads:
        load.start()

    barrier = pltpu.get_barrier_semaphore()
    y_peers = [lax.rem(y + d, NY) for d in (1, 3, 2)]
    x_peers = [
        (lax.rem(x + dx, NX), lax.rem(c + dc, NC))
        for dx in (2, 1, 3, 0)
        for dc in (0, 1)
        if dx + dc > 0
    ]

    def greet(step, _):
        oz = lax.rem(z + lax.div(step, NY), NZ)
        oy = lax.rem(y + lax.rem(step, NY), NY)
        pl.semaphore_signal(barrier, inc=1, device_id=device(x, oz, c, oy), device_id_type=MESH)
        return 0

    lax.fori_loop(1, peers, greet, 0)
    for ox, oc in x_peers:
        pl.semaphore_signal(barrier, inc=1, device_id=device(ox, z, oc, y), device_id_type=MESH)

    lanes_of = lax.broadcasted_iota(jnp.int32, (LOCAL, 128), 1)
    frame_of = lax.broadcasted_iota(jnp.int32, (LOCAL, 128), 0)
    spread = (lax.rem(lanes_of, LOCAL) == frame_of).astype(jnp.float32)
    kept = jnp.dot(flags[...].astype(jnp.float32), spread, preferred_element_type=jnp.float32)
    for i in range(NY):
        live[i] = jnp.broadcast_to(kept[i : i + 1], (16, 128)).astype(jnp.bfloat16)
    line[:, :, 0:LOCAL] = jnp.zeros((2, 2, LOCAL, 16, INNER), jnp.bfloat16)
    loads[0].wait()

    def unpick(step, _):
        p, g = lax.div(step, LOCAL), lax.rem(step, LOCAL)
        start = pl.multiple_of(g * CHANNELS, CHANNELS)
        pieces = [volts[p, :, pl.ds(start + a * INNER, INNER)] for a in range(16)]
        frame = jnp.swapaxes(jnp.stack(pieces, axis=0), 0, 1)
        for i in range(8):
            stage[i, p, g] = frame[i]
        return 0

    lax.fori_loop(0, 2 * LOCAL, unpick, 0)
    pl.semaphore_wait(barrier, peers - 1 + len(x_peers))

    here = pl.ds(LOCAL + LOCAL * y, LOCAL)
    for other in y_peers:
        pltpu.make_async_remote_copy(
            src_ref=live.at[other], dst_ref=marks.at[y], send_sem=f_send, recv_sem=f_recv,
            device_id=device(x, z, c, other), device_id_type=MESH,
        ).start()
    pltpu.make_async_copy(live.at[y], marks.at[y], f_recv).start()

    def share(j):
        for p in range(2):
            for other in y_peers:
                pltpu.make_async_remote_copy(
                    src_ref=stage.at[2 * other + j, p], dst_ref=line.at[j, p, here],
                    send_sem=y_send, recv_sem=y_recv.at[2 * j + p],
                    device_id=device(x, z, c, other), device_id_type=MESH,
                ).start()
            pltpu.make_async_copy(
                stage.at[2 * y + j, p], line.at[j, p, here], y_recv.at[2 * j + p]
            ).start()

    def sift(j, p, begin, groups):
        for half in range(2):
            lanes = slice(128 * half, 128 * half + 128)

            def step(index, _):
                base = begin + index * 8
                taps = [window[t, :, lanes] for t in range(TAPS)]
                total = [None] * 8
                for u in range(8 + TAPS - 1):
                    value = line[j, p, base + 1 + u, :, lanes].astype(jnp.float32)
                    for g in range(8):
                        t = u - g
                        if 0 <= t < TAPS:
                            term = taps[t] * value
                            total[g] = term if t == 0 else total[g] + term
                for g in range(8):
                    filtered[base + g, p, :, lanes] = total[g].astype(jnp.bfloat16)
                return 0

            lax.fori_loop(0, groups, step, 0)

    def transform(part, j):
        reals, imags = [], []
        for half in range(2):
            block = filtered[pl.ds(part * LOCAL + 8 * half, 8)].reshape(256, INNER)
            value = jnp.dot(first[...], block, preferred_element_type=jnp.float32)
            real, imag = value[:128], value[128:]
            rot_real = real * cosine[...] + imag * sine[...]
            rot_imag = imag * cosine[...] - real * sine[...]
            reals.append(rot_real.reshape(16, 8, INNER))
            imags.append(rot_imag.reshape(16, 8, INNER))
        real = jnp.concatenate(reals, axis=1).reshape(256, INNER)
        imag = jnp.concatenate(imags, axis=1).reshape(256, INNER)
        rotated = jnp.concatenate([real, imag], axis=1).astype(jnp.bfloat16)
        out = lax.dot_general(
            second[...], rotated, (((1,), (1,)), ((), ())), preferred_element_type=jnp.float32
        )
        keep = marks[part][0:1].astype(jnp.float32)
        out = out * jnp.concatenate([keep, keep], axis=1)
        out = out.astype(jnp.bfloat16).reshape(NX * NC, 2, 2, NZ, 256)
        for yy in range(NY):
            low = 128 * (yy % 2)
            spectra[pl.ds((4 * j + yy) * 8, 8), part] = out[:, yy // 2, :, :, low : low + 128]

    def wait(ref, sem):
        pltpu.make_async_copy(ref, ref, sem).wait()

    def arrived(j, p):
        wait(line.at[j, p, pl.ds(LOCAL, FRAMES)], y_recv.at[2 * j + p])

    def produce(j):
        def step(part, _):
            sift(j, 1, part * LOCAL, 2)
            transform(part, j)
            return 0

        lax.fori_loop(0, 4, step, 0)

    def cross(j, dy):
        base = (4 * j + lax.rem(y + dy, NY)) * 8
        for ox, oc in x_peers:
            pltpu.make_async_remote_copy(
                src_ref=spectra.at[base + 2 * ox + oc], dst_ref=turned[j][dy].at[x, c],
                send_sem=x_send, recv_sem=x_recv.at[4 * j + dy],
                device_id=device(ox, z, oc, y), device_id_type=MESH,
            ).start()
        pltpu.make_async_copy(
            spectra.at[base + 2 * x + c], turned[j][dy].at[x, c], x_recv.at[4 * j + dy]
        ).start()

    def forward(j, dy):
        oy = lax.rem(y + dy, NY)
        wait(turned[j][dy], x_recv.at[4 * j + dy])
        if dy < 2:
            cross(j, dy + 2)
        for m in range(count):
            which = plan[zh * 4 + m]
            piece = turned[j][dy][which].astype(jnp.float32)
            board[m] = piece.reshape(256, 128)
            for oz in range(NZ):
                rows = board[m, pl.ds(oz, 16, stride=16), :]
                ready[j, oz * NY + oy, m] = rows.astype(jnp.bfloat16)

        def send(step, _):
            far = 8 - lax.div(step + 1, 2)
            oz = lax.rem(z + NZ + (2 * lax.rem(step, 2) - 1) * far, NZ)
            pltpu.make_async_remote_copy(
                src_ref=ready.at[j, oz * NY + oy], dst_ref=landed[j].at[zh, zl, :, y],
                send_sem=z_send, recv_sem=z_recv.at[j],
                device_id=device(x, oz, c, oy), device_id_type=MESH,
            ).start()
            return 0

        lax.fori_loop(0, NZ - 1, send, 0)
        source, target = ready.at[j, z * NY + oy], landed[j].at[zh, zl, :, y]
        if dy == 0:
            pltpu.make_async_copy(source, target, z_recv.at[j]).start()
        else:
            pltpu.make_async_remote_copy(
                src_ref=source, dst_ref=target, send_sem=z_send, recv_sem=z_recv.at[j],
                device_id=device(x, z, c, oy), device_id_type=MESH,
            ).start()

    share(0)
    for load in loads[1:]:
        load.wait()
    for j in range(2):
        arrived(j, 0)
        if j == 0:
            share(1)
        sift(j, 0, 0, 8)
        arrived(j, 1)
        if j == 0:
            wait(marks, f_recv)
        produce(j)
        cross(j, 0)
        cross(j, 1)
        if j == 0:
            forward(0, 0)
            forward(0, 1)
    forward(0, 2)
    forward(0, 3)
    for dy in range(NY):
        forward(1, dy)

    wait(live.at[pl.ds(0, 3)], f_send)
    wait(stage.at[pl.ds(0, 6)], y_send)
    wait(spectra.at[pl.ds(0, 56)], x_send)

    for j in range(2):
        wait(landed[j], z_recv.at[j])
        for slot in range(4):
            quarter, spot = plan[16 + slot], plan[20 + slot]
            value = landed[j][quarter, :, spot].astype(jnp.float32)
            for i in range(4):
                for core in range(NC):
                    for t in range(NY):
                        row = ((i * NC + core) * NY + t) * 2 + j
                        pairing[slot, pl.ds(8 * row, 8), :] = value[i, t, 8 * core : 8 * core + 8]

    lane = lax.broadcasted_iota(jnp.int32, (1, 128), 1)

    def side(slot):
        return [
            [pairing[slot, pl.ds(2 * g + part, 64, stride=8), :] for g in range(4)]
            for part in range(2)
        ]

    for b in range(2):
        left = side(2 * b)
        lefts = []
        for channel in range(8):
            keep = (lax.div(lane, 16) == channel).astype(jnp.float32)
            lefts.append(
                jnp.concatenate([(v * keep).astype(jnp.bfloat16) for v in left[0] + left[1]], axis=1)
            )
        left = jnp.concatenate(lefts, axis=0)
        right = side(2 * b + 1)
        upper = jnp.concatenate(right[0] + right[1], axis=1)
        lower = jnp.concatenate([-v for v in right[1]] + right[0], axis=1)
        right = jnp.concatenate([upper, lower], axis=0).astype(jnp.bfloat16)
        value = lax.dot_general(
            left, right, (((1,), (1,)), ((), ())), preferred_element_type=jnp.float32
        )
        result[:, b] = (value * (1.0 / FRAMES)).reshape(8, BLOCK, 2 * BLOCK)

    sent = ready.at[:, pl.ds(0, peers - 1)]
    wait(sent, z_send)


def vmem():
    return pl.BlockSpec(memory_space=pltpu.VMEM)


def smem():
    return pl.BlockSpec(memory_space=pltpu.SMEM)


def far():
    return pl.BlockSpec(memory_space=pl.ANY)


def whole(count, plan, volts, flags):
    bf16, f32 = jnp.bfloat16, jnp.float32
    cosine, sine = twiddle_tables()
    return pl.pallas_call(
        functools.partial(whole_kernel, count),
        out_shape=jax.ShapeDtypeStruct((8, 2, BLOCK, 2 * BLOCK), f32),
        in_specs=[smem(), far(), vmem()] + [far()] * 5,
        out_specs=vmem(),
        scratch_shapes=[
            pltpu.VMEM((2, 8, LOCAL * CHANNELS), bf16),
            pltpu.VMEM((TAPS, 16, INNER), f32),
            pltpu.VMEM((256, 256), bf16),
            pltpu.VMEM((128, INNER), f32),
            pltpu.VMEM((128, INNER), f32),
            pltpu.VMEM((512, 512), bf16),
            pltpu.VMEM((8, 2, LOCAL, 16, INNER), bf16),
            pltpu.VMEM((2, 2, LOCAL + FRAMES, 16, INNER), bf16),
            pltpu.VMEM((NY, 16, 128), bf16),
            pltpu.VMEM((NY, 16, 128), bf16),
            pltpu.VMEM((FRAMES, 2, 16, INNER), bf16),
            pltpu.VMEM((64, 4, 2, NZ, 128), bf16),
        ]
        + [pltpu.VMEM((NX, NC, 4, 2, NZ, 128), bf16)] * 8
        + [
            pltpu.VMEM((count, 256, 128), f32),
            pltpu.VMEM((4, 512, 128), f32),
            pltpu.VMEM((2, NZ * NY, count, 16, 128), bf16),
            pltpu.VMEM((4, 4, count, NY, 16, 128), bf16),
            pltpu.VMEM((4, 4, count, NY, 16, 128), bf16),
            pltpu.SemaphoreType.DMA((6,)),
            pltpu.SemaphoreType.DMA,
            pltpu.SemaphoreType.DMA,
            pltpu.SemaphoreType.DMA,
            pltpu.SemaphoreType.DMA((4,)),
            pltpu.SemaphoreType.DMA,
            pltpu.SemaphoreType.DMA((8,)),
            pltpu.SemaphoreType.DMA,
            pltpu.SemaphoreType.DMA((2,)),
        ],
        compiler_params=pltpu.CompilerParams(
            collective_id=count - 1, has_side_effects=True, vmem_limit_bytes=44 << 20
        ),
        name="whole",
    )(
        plan, volts, flags, jnp.asarray(window_table()), jnp.asarray(first_table()),
        jnp.asarray(cosine), jnp.asarray(sine), jnp.asarray(second_table()),
    )


def local(voltages, flags, pairs):
    plan, rounds = pl.pallas_call(
        plan_kernel,
        out_shape=(
            jax.ShapeDtypeStruct((24,), jnp.int32),
            jax.ShapeDtypeStruct((1,), jnp.int32),
        ),
        in_specs=[smem()],
        out_specs=(smem(), smem()),
        name="plan",
    )(pairs)
    branches = [functools.partial(whole, m) for m in range(1, 5)]
    return lax.switch(rounds[0], branches, plan, voltages, flags)


def solution(mesh):
    placed = (P(None, "chan", "tm"), P("chan", "tm"), P())
    return jax.shard_map(
        local,
        mesh=mesh,
        in_specs=placed,
        out_specs=P(("chan", "tm"), None, None, None),
        check_vma=False,
    )
```

```python
import functools
import math

import jax
import jax.numpy as jnp
import ml_dtypes
import numpy as np
from jax import lax
from jax.experimental import pallas as pl
from jax.experimental.pallas import tpu as pltpu
from jax.sharding import PartitionSpec as P

CHANNELS = 4096
TAPS = 16
BLOCK = 64
NX, NZ, NC, NY = 4, 16, 2, 4
LOCAL = 16
FRAMES = 64
INNER = 256
MESH = pl.DeviceIdType.MESH


def window_table():
    length = TAPS * CHANNELS
    index = np.arange(length, dtype=np.float64)
    offset = (index - length / 2 + 0.5) / CHANNELS
    taper = 0.5 - 0.5 * np.cos(2.0 * math.pi * (index + 0.5) / length)
    return (np.sinc(offset) * taper).astype(np.float32).reshape(TAPS, 16, INNER)


def dft_table(order, factor):
    counts = np.arange(order)
    angle = (counts[:, None] * counts[None, :] % order).astype(np.float64) * (2.0 * math.pi / order)
    cosine = np.cos(angle) * factor
    sine = np.sin(angle) * factor
    upper = np.stack([cosine, -sine], axis=1)
    lower = np.stack([sine, cosine], axis=1)
    table = np.stack([upper, lower], axis=0)
    return table.astype(np.float32).astype(ml_dtypes.bfloat16)


def first_table():
    first = dft_table(16, 0.25).astype(np.float32)
    table = np.zeros((2, 16, 8, 8, 2, 16), np.float32)
    for f in range(8):
        table[:, :, f, f] = first.transpose(2, 3, 0, 1)
    return table.reshape(256, 256).astype(ml_dtypes.bfloat16)


def twiddle_tables():
    angle = np.arange(16)[:, None] * np.arange(INNER)[None, :] * (2.0 * math.pi / CHANNELS)
    angle = np.repeat(angle, 8, axis=0)
    return np.cos(angle).astype(np.float32), np.sin(angle).astype(np.float32)


def second_table():
    second = dft_table(INNER, 1.0 / math.sqrt(INNER))
    second = second.transpose(3, 2, 0, 1).reshape(NX, NZ, NC, 2, 2, 2 * INNER)
    return np.ascontiguousarray(second.transpose(0, 2, 3, 4, 1, 5)).reshape(2 * INNER, 2 * INNER)


def place():
    chan = lax.axis_index("chan")
    return (
        lax.div(chan, NZ * NC),
        lax.rem(lax.div(chan, NC), NZ),
        lax.rem(chan, NC),
        lax.axis_index("tm"),
    )


def device(x, z, c, y):
    return ((x * NZ + z) * NC + c, y)


def plan_kernel(pairs_ref, plan_ref, rounds_ref):
    zero, one = jnp.int32(0), jnp.int32(1)
    block = [pairs_ref[s // 2, s % 2] for s in range(4)]
    across = [lax.div(b, 4) for b in block]
    quarter = [lax.rem(b, 4) for b in block]
    fresh, order = [], []
    for s in range(4):
        new, spot = one, zero
        for e in range(s):
            spot = spot + jnp.where(quarter[e] == quarter[s], fresh[e], zero)
        for e in range(s):
            same = block[e] == block[s]
            spot = jnp.where(same, order[e], spot)
            new = jnp.where(same, zero, new)
        fresh.append(new)
        order.append(spot)
    most, crowded, alone = zero, zero, zero
    for q in range(4):
        count = zero
        for s in range(4):
            count = count + jnp.where(quarter[s] == q, fresh[s], zero)
        most = jnp.maximum(most, count)
        crowded = crowded + jnp.where(count > 1, one, zero)
        alone = jnp.where(count > 1, jnp.int32(q), alone)
        for m in range(4):
            pick = zero
            for s in range(4):
                hit = (quarter[s] == q) & (order[s] == m)
                pick = jnp.where(hit, across[s], pick)
            plan_ref[4 * q + m] = pick
    single = (most == 2) & (crowded == 1)
    for s in range(4):
        extra = jnp.where(order[s] == 0, quarter[s], jnp.int32(4))
        plan_ref[16 + s] = jnp.where(single, extra, order[s])
        plan_ref[20 + s] = jnp.where(single, zero, quarter[s])
    form = jnp.where(most == 1, zero, jnp.where(most == 2, one, jnp.int32(6)))
    rounds_ref[0] = jnp.where(single, 2 + alone, form)


def whole_kernel(
    count, only, plan, volts_in, flags, window_in, first_in, cosine_in, sine_in, second_in,
    result,
    volts, window, first, cosine, sine, second,
    stage, line, live, marks, filtered, spectra,
    t0, t1, t2, t3, t4, t5, t6, t7,
    board, pairing, ready, landed_a, landed_b,
    in_sem, f_send, f_recv, y_send, y_recv, x_send, x_recv, z_send, z_recv,
):
    turned = ((t0, t1, t2, t3), (t4, t5, t6, t7))
    landed = (landed_a, landed_b)
    x, z, c, y = place()
    zh, zl = lax.div(z, 4), lax.rem(z, 4)
    peers = NZ * NY
    turns, width = (1, count) if only is None else (2, 1)

    loads = [
        pltpu.make_async_copy(source, target, in_sem.at[i])
        for i, (source, target) in enumerate(
            [
                (volts_in.at[0], volts.at[0]), (volts_in.at[1], volts.at[1]),
                (window_in, window), (first_in, first),
                (cosine_in, cosine), (sine_in, sine), (second_in, second),
            ]
        )
    ]
    for load in loads:
        load.start()

    barrier = pltpu.get_barrier_semaphore()
    y_peers = [lax.rem(y + d, NY) for d in (1, 3, 2)]
    x_peers = [
        (lax.rem(x + dx, NX), lax.rem(c + dc, NC))
        for dx in (2, 1, 3, 0)
        for dc in (0, 1)
        if dx + dc > 0
    ]

    def greet(step, _):
        oz = lax.rem(z + lax.div(step, NY), NZ)
        oy = lax.rem(y + lax.rem(step, NY), NY)
        pl.semaphore_signal(barrier, inc=1, device_id=device(x, oz, c, oy), device_id_type=MESH)
        return 0

    lax.fori_loop(1, peers, greet, 0)
    for ox, oc in x_peers:
        pl.semaphore_signal(barrier, inc=1, device_id=device(ox, z, oc, y), device_id_type=MESH)

    lanes_of = lax.broadcasted_iota(jnp.int32, (LOCAL, 128), 1)
    frame_of = lax.broadcasted_iota(jnp.int32, (LOCAL, 128), 0)
    spread = (lax.rem(lanes_of, LOCAL) == frame_of).astype(jnp.float32)
    kept = jnp.dot(flags[...].astype(jnp.float32), spread, preferred_element_type=jnp.float32)
    for i in range(NY):
        live[i] = jnp.broadcast_to(kept[i : i + 1], (16, 128)).astype(jnp.bfloat16)
    line[:, :, 0:LOCAL] = jnp.zeros((2, 2, LOCAL, 16, INNER), jnp.bfloat16)

    def unpick(p):
        loads[p].wait()

        def step(g, _):
            start = pl.multiple_of(g * CHANNELS, CHANNELS)
            pieces = [volts[p, :, pl.ds(start + a * INNER, INNER)] for a in range(16)]
            frame = jnp.swapaxes(jnp.stack(pieces, axis=0), 0, 1)
            for i in range(8):
                stage[i, p, g] = frame[i]
            return 0

        lax.fori_loop(0, LOCAL, step, 0)

    unpick(0)
    pl.semaphore_wait(barrier, peers - 1 + len(x_peers))

    here = pl.ds(LOCAL + LOCAL * y, LOCAL)
    def share(j, p):
        for other in y_peers:
            pltpu.make_async_remote_copy(
                src_ref=stage.at[2 * other + j, p], dst_ref=line.at[j, p, here],
                send_sem=y_send, recv_sem=y_recv.at[2 * j + p],
                device_id=device(x, z, c, other), device_id_type=MESH,
            ).start()
        pltpu.make_async_copy(
            stage.at[2 * y + j, p], line.at[j, p, here], y_recv.at[2 * j + p]
        ).start()

    share(0, 0)
    unpick(1)
    share(0, 1)
    for other in y_peers:
        pltpu.make_async_remote_copy(
            src_ref=live.at[other], dst_ref=marks.at[y], send_sem=f_send, recv_sem=f_recv,
            device_id=device(x, z, c, other), device_id_type=MESH,
        ).start()
    pltpu.make_async_copy(live.at[y], marks.at[y], f_recv).start()

    def sift(j, p, begin, groups):
        for half in range(2):
            lanes = slice(128 * half, 128 * half + 128)

            def step(index, _):
                base = begin + index * 8
                taps = [window[t, :, lanes] for t in range(TAPS)]
                total = [None] * 8
                for u in range(8 + TAPS - 1):
                    value = line[j, p, base + 1 + u, :, lanes].astype(jnp.float32)
                    for g in range(8):
                        t = u - g
                        if 0 <= t < TAPS:
                            term = taps[t] * value
                            total[g] = term if t == 0 else total[g] + term
                for g in range(8):
                    filtered[base + g, p, :, lanes] = total[g].astype(jnp.bfloat16)
                return 0

            lax.fori_loop(0, groups, step, 0)

    def transform(part, j):
        reals, imags = [], []
        for half in range(2):
            block = filtered[pl.ds(part * LOCAL + 8 * half, 8)].reshape(256, INNER)
            value = jnp.dot(first[...], block, preferred_element_type=jnp.float32)
            real, imag = value[:128], value[128:]
            rot_real = real * cosine[...] + imag * sine[...]
            rot_imag = imag * cosine[...] - real * sine[...]
            reals.append(rot_real.reshape(16, 8, INNER))
            imags.append(rot_imag.reshape(16, 8, INNER))
        real = jnp.concatenate(reals, axis=1).reshape(256, INNER)
        imag = jnp.concatenate(imags, axis=1).reshape(256, INNER)
        rotated = jnp.concatenate([real, imag], axis=1).astype(jnp.bfloat16)
        out = lax.dot_general(
            second[...], rotated, (((1,), (1,)), ((), ())), preferred_element_type=jnp.float32
        )
        keep = marks[part][0:1].astype(jnp.float32)
        out = out * jnp.concatenate([keep, keep], axis=1)
        out = out.astype(jnp.bfloat16).reshape(NX * NC, 2, 2, NZ, 256)
        for yy in range(NY):
            low = 128 * (yy % 2)
            spectra[pl.ds((4 * j + yy) * 8, 8), part] = out[:, yy // 2, :, :, low : low + 128]

    def wait(ref, sem):
        pltpu.make_async_copy(ref, ref, sem).wait()

    def arrived(j, p):
        wait(line.at[j, p, pl.ds(LOCAL, FRAMES)], y_recv.at[2 * j + p])

    def produce(j):
        def step(part, _):
            sift(j, 1, part * LOCAL, 2)
            transform(part, j)
            return 0

        lax.fori_loop(0, 4, step, 0)

    def cross(j, dy):
        base = (4 * j + lax.rem(y + dy, NY)) * 8
        for ox, oc in x_peers:
            pltpu.make_async_remote_copy(
                src_ref=spectra.at[base + 2 * ox + oc], dst_ref=turned[j][dy].at[x, c],
                send_sem=x_send, recv_sem=x_recv.at[4 * j + dy],
                device_id=device(ox, z, oc, y), device_id_type=MESH,
            ).start()
        pltpu.make_async_copy(
            spectra.at[base + 2 * x + c], turned[j][dy].at[x, c], x_recv.at[4 * j + dy]
        ).start()

    def forward(j, dy):
        oy = lax.rem(y + dy, NY)
        wait(turned[j][dy], x_recv.at[4 * j + dy])
        if dy < 2:
            cross(j, dy + 2)

        def hand_on(turn):
            for w in range(width):
                which = plan[zh * 4 + turn + w]
                piece = turned[j][dy][which].astype(jnp.float32)
                board[turn + w] = piece.reshape(256, 128)
                for oz in range(NZ):
                    rows = board[turn + w, pl.ds(oz, 16, stride=16), :]
                    ready[j, turn, oz * NY + oy, w] = rows.astype(jnp.bfloat16)
            if only is None:
                target = landed[j].at[:, zh, zl, y]
            else:
                target = landed[j].at[pl.ds(4 if turn else zh, 1), 0, zl, y]

            def send(step, _):
                far = 8 - lax.div(step + 1, 2)
                oz = lax.rem(z + NZ + (2 * lax.rem(step, 2) - 1) * far, NZ)
                pltpu.make_async_remote_copy(
                    src_ref=ready.at[j, turn, oz * NY + oy], dst_ref=target,
                    send_sem=z_send.at[turn], recv_sem=z_recv.at[j],
                    device_id=device(x, oz, c, oy), device_id_type=MESH,
                ).start()
                return 0

            lax.fori_loop(0, NZ - 1, send, 0)
            source = ready.at[j, turn, z * NY + oy]
            if dy == 0:
                pltpu.make_async_copy(source, target, z_recv.at[j]).start()
            else:
                pltpu.make_async_remote_copy(
                    src_ref=source, dst_ref=target,
                    send_sem=z_send.at[turn], recv_sem=z_recv.at[j],
                    device_id=device(x, z, c, oy), device_id_type=MESH,
                ).start()

        hand_on(0)
        if only is not None:
            pl.when(zh == only)(lambda: hand_on(1))

    for load in loads[2:]:
        load.wait()
    for j in range(2):
        arrived(j, 0)
        if j == 0:
            share(1, 0)
            share(1, 1)
        sift(j, 0, 0, 8)
        arrived(j, 1)
        if j == 0:
            wait(marks, f_recv)
        produce(j)
        cross(j, 0)
        cross(j, 1)
        if j == 0:
            forward(0, 0)
            forward(0, 1)
    forward(0, 2)
    forward(0, 3)
    for dy in range(NY):
        forward(1, dy)

    wait(live.at[pl.ds(0, 3)], f_send)
    wait(stage.at[pl.ds(0, 6)], y_send)
    wait(spectra.at[pl.ds(0, 56)], x_send)

    for j in range(2):
        wait(landed[j], z_recv.at[j])
        for slot in range(4):
            value = landed[j][plan[16 + slot], plan[20 + slot]].astype(jnp.float32)
            for i in range(4):
                for core in range(NC):
                    for t in range(NY):
                        row = ((i * NC + core) * NY + t) * 2 + j
                        pairing[slot, pl.ds(8 * row, 8), :] = value[i, t, 8 * core : 8 * core + 8]

    lane = lax.broadcasted_iota(jnp.int32, (1, 128), 1)

    def side(slot):
        return [
            [pairing[slot, pl.ds(2 * g + part, 64, stride=8), :] for g in range(4)]
            for part in range(2)
        ]

    for b in range(2):
        left = side(2 * b)
        lefts = []
        for channel in range(8):
            keep = (lax.div(lane, 16) == channel).astype(jnp.float32)
            lefts.append(
                jnp.concatenate([(v * keep).astype(jnp.bfloat16) for v in left[0] + left[1]], axis=1)
            )
        left = jnp.concatenate(lefts, axis=0)
        right = side(2 * b + 1)
        upper = jnp.concatenate(right[0] + right[1], axis=1)
        lower = jnp.concatenate([-v for v in right[1]] + right[0], axis=1)
        right = jnp.concatenate([upper, lower], axis=0).astype(jnp.bfloat16)
        value = lax.dot_general(
            left, right, (((1,), (1,)), ((), ())), preferred_element_type=jnp.float32
        )
        result[:, b] = (value * (1.0 / FRAMES)).reshape(8, BLOCK, 2 * BLOCK)

    wait(ready.at[:, 0, pl.ds(0, peers - 1)], z_send.at[0])
    if only is not None:
        pl.when(zh == only)(lambda: wait(ready.at[:, 1, pl.ds(0, peers - 1)], z_send.at[1]))


def vmem():
    return pl.BlockSpec(memory_space=pltpu.VMEM)


def smem():
    return pl.BlockSpec(memory_space=pltpu.SMEM)


def far():
    return pl.BlockSpec(memory_space=pl.ANY)


def whole(count, only, ident, plan, volts, flags):
    bf16, f32 = jnp.bfloat16, jnp.float32
    cosine, sine = twiddle_tables()
    turns, width = (1, count) if only is None else (2, 1)
    landing = (count, 4, 4, NY, 16, 128) if only is None else (5, 1, 4, NY, 16, 128)
    return pl.pallas_call(
        functools.partial(whole_kernel, count, only),
        out_shape=jax.ShapeDtypeStruct((8, 2, BLOCK, 2 * BLOCK), f32),
        in_specs=[smem(), far(), vmem()] + [far()] * 5,
        out_specs=vmem(),
        scratch_shapes=[
            pltpu.VMEM((2, 8, LOCAL * CHANNELS), bf16),
            pltpu.VMEM((TAPS, 16, INNER), f32),
            pltpu.VMEM((256, 256), bf16),
            pltpu.VMEM((128, INNER), f32),
            pltpu.VMEM((128, INNER), f32),
            pltpu.VMEM((512, 512), bf16),
            pltpu.VMEM((8, 2, LOCAL, 16, INNER), bf16),
            pltpu.VMEM((2, 2, LOCAL + FRAMES, 16, INNER), bf16),
            pltpu.VMEM((NY, 16, 128), bf16),
            pltpu.VMEM((NY, 16, 128), bf16),
            pltpu.VMEM((FRAMES, 2, 16, INNER), bf16),
            pltpu.VMEM((64, 4, 2, NZ, 128), bf16),
        ]
        + [pltpu.VMEM((NX, NC, 4, 2, NZ, 128), bf16)] * 8
        + [
            pltpu.VMEM((count, 256, 128), f32),
            pltpu.VMEM((4, 512, 128), f32),
            pltpu.VMEM((2, turns, NZ * NY, width, 16, 128), bf16),
            pltpu.VMEM(landing, bf16),
            pltpu.VMEM(landing, bf16),
            pltpu.SemaphoreType.DMA((7,)),
            pltpu.SemaphoreType.DMA,
            pltpu.SemaphoreType.DMA,
            pltpu.SemaphoreType.DMA,
            pltpu.SemaphoreType.DMA((4,)),
            pltpu.SemaphoreType.DMA,
            pltpu.SemaphoreType.DMA((8,)),
            pltpu.SemaphoreType.DMA((turns,)),
            pltpu.SemaphoreType.DMA((2,)),
        ],
        compiler_params=pltpu.CompilerParams(
            collective_id=ident, has_side_effects=True, vmem_limit_bytes=44 << 20
        ),
        name="whole",
    )(
        plan, volts, flags, jnp.asarray(window_table()), jnp.asarray(first_table()),
        jnp.asarray(cosine), jnp.asarray(sine), jnp.asarray(second_table()),
    )


def local(voltages, flags, pairs):
    plan, rounds = pl.pallas_call(
        plan_kernel,
        out_shape=(
            jax.ShapeDtypeStruct((24,), jnp.int32),
            jax.ShapeDtypeStruct((1,), jnp.int32),
        ),
        in_specs=[smem()],
        out_specs=(smem(), smem()),
        name="plan",
    )(pairs)
    forms = [(1, None), (2, None), (2, 0), (2, 1), (2, 2), (2, 3), (4, None)]
    branches = [functools.partial(whole, *form, ident) for ident, form in enumerate(forms)]
    return lax.switch(rounds[0], branches, plan, voltages, flags)


def solution(mesh):
    placed = (P(None, "chan", "tm"), P("chan", "tm"), P())
    return jax.shard_map(
        local,
        mesh=mesh,
        in_specs=placed,
        out_specs=P(("chan", "tm"), None, None, None),
        check_vma=False,
    )
```
